32 devices in a mesh: dp: 8 (over z, core), tensor: 4 (over y, x).
Axes of the slice: x: 2, y: 2, z: 4, core: 2. Of those that a mesh axis runs over, the one named last changes fastest.
Arguments:
- inputs: bfloat16 [2048, 6144], P('dp'), may hold values from -6 to 6
- grad_hidden: bfloat16 [2048, 24576], P('dp', 'tensor'), may hold values from -6 to 6
- w_blocks: bfloat16 [4, 1152, 128, 128], P('tensor', 'dp'), may hold values from -0.15625 to 0.15625
- block_ids: int32 [4, 1152], P('tensor', 'dp'), may hold values from 0 to 2303, as said below
- counts: int32 [4, 8], P('tensor', 'dp'), may hold values from 1 to 144, 576 in all within a row
Outputs:
- hidden: bfloat16 [2048, 24576], P('dp', 'tensor')
- grad_inputs: bfloat16 [2048, 6144], P('dp', 'tensor')
- grad_blocks: bfloat16 [4, 1152, 128, 128], P('tensor', 'dp')
The draws below stay inside these ranges and needn't reach their ends.
Inputs may be any that keep to these rules, and one draw needn't show every extreme that they name: `block_ids`: within one tensor index all 1152 ids are distinct. Each row of counts sums to 576.
All inputs are finite; a program needn't handle non-finite values. No bound on the sum of `counts` on one device may be relied on, other than what follows from the above.
Results may differ from the reference program's by a relative error of at most 0.023.
Values may be sent and summed in bfloat16 or wider, within the bound.
No kernel may reach another device: no remote copies, remote signals or barrier semaphores. Data moves between devices by JAX's collectives and lax.ppermute only.
A program may use at most 192 MiB of HBM per device.

```python
import math
import jax
import jax.numpy as jnp
import numpy as np
from jax import lax

D = 6144
FF = 24576
BLK = 128
TOK_DEV = 256
TOKENS = 2048
FF_DEV = 6144
RB = 48
CB = 48
NBLK = 2304
NNZ = 576
CAP = 144
SLOTS = 1152
N_DP = 8
N_TENSOR = 4


def draw_block_ids(key, part):
    row_keys = jax.random.split(key, N_TENSOR)

    def one_row(row_key):
        return jax.random.permutation(row_key, NBLK)[:SLOTS]
    return jax.vmap(one_row)(row_keys).astype(jnp.int32)


def level_of(stream_key, extent, cuts, smallest, high):
    gain, own = 1.0, jax.random.fold_in(stream_key, 6)
    for dim, parts in cuts:
        steps = jnp.exp(jax.random.uniform(jax.random.fold_in(own, dim), (parts,), jnp.float32, smallest / len(cuts), high / len(cuts)))
        gain = gain * jnp.repeat(steps, extent[dim] // parts).reshape([-1 if axis == dim else 1 for axis in range(len(extent))])
    return gain


def length_profile(count, total, limit, lean):
    weights = [(1 << 20) // math.isqrt(rank ** lean) + 1 for rank in range(2, count + 1)]
    surplus, given = total - limit - (count - 1), [1] * (count - 1)
    while surplus > 0:
        candidates = [i for i in range(count - 1) if given[i] < limit]
        pool, remaining = sum([weights[i] for i in candidates]), surplus
        for i in candidates:
            addition = min(limit - given[i], max(1, remaining * weights[i] // pool), surplus)
            given[i] = given[i] + addition
            surplus = surplus - addition
    return np.array([limit] + given)


def uneven_parts(key, count, total, most, lean):
    if count == 2:
        one = jax.random.randint(key, (), max(1, total - most), min(most, total - 1) + 1)
        return jnp.stack([one, total - one])
    tallies = jnp.asarray(length_profile(count, total, most, lean), jnp.int32)
    pairs = (count - 1) // 2
    source_of, sink = tallies[1:1 + 2 * pairs:2], tallies[2:2 + 2 * pairs:2]
    margin = jnp.minimum(source_of - 1, most - sink)
    shifted = jax.random.randint(jax.random.fold_in(key, 1), (pairs,), 0, 1 << 20) % (margin + 1)
    tallies = tallies.at[1:1 + 2 * pairs:2].set(source_of - shifted).at[2:2 + 2 * pairs:2].set(sink + shifted)
    return tallies[jax.random.permutation(jax.random.fold_in(key, 2), count)]


def gaussian(stream_key, extent, spread, limit, cuts=(), kind=jnp.bfloat16):
    gain = level_of(stream_key, extent, cuts, -0.22, 0.18) if cuts else 1.0
    entries = jax.random.normal(stream_key, extent, jnp.float32) * spread * gain
    return jnp.minimum(jnp.maximum(entries, -limit), limit).astype(kind)


def setup_inputs(seed: int = 0) -> dict:
    arg_keys = jax.random.split(jax.random.key(seed), 6)
    return {
        "inputs": gaussian(arg_keys[0], (TOKENS, D), 1.0, 6.0, ((0, 8),)),
        "grad_hidden": gaussian(arg_keys[1], (TOKENS, FF), 1.0, 6.0, ((0, 8), (1, 4))),
        "w_blocks": gaussian(arg_keys[2], (N_TENSOR, SLOTS, BLK, BLK), (D // 4) ** -0.5, 0.15625, ((0, 4), (1, 8))),
        "block_ids": draw_block_ids(jax.random.fold_in(arg_keys[5], 71), 0),
        "counts": jax.vmap(lambda own: uneven_parts(own, N_DP, NNZ, CAP, 2))(jax.random.split(arg_keys[4], N_TENSOR)).reshape((N_TENSOR, N_DP)).astype(jnp.int32),
    }


GELU_C = 0.7978845608028654
GELU_A = 0.044715

def gelu_value(values):
    inner_arg = GELU_C * (values + GELU_A * values * values * values)
    return 0.5 * values * (1.0 + jnp.tanh(inner_arg))

def gelu_slope(values):
    inner_arg = GELU_C * (values + GELU_A * values * values * values)
    tanh_value = jnp.tanh(inner_arg)
    return 0.5 * (1.0 + tanh_value) + 0.5 * values * (1.0 - tanh_value * tanh_value) * GELU_C * (1.0 + 3.0 * GELU_A * values * values)

def shard_pass(x_blocks, x_groups, blocks, ids_row, owner_counts, grad_cols):
    slot_index = jnp.arange(SLOTS, dtype=jnp.int32)
    is_live = slot_index % CAP < owner_counts[slot_index // CAP]
    live_order = jnp.argsort(jnp.where(is_live, 0, 1).astype(jnp.int32), stable=True)[:NNZ].astype(jnp.int32)
    live_ids = ids_row[live_order].astype(jnp.int32)
    row_index = (live_ids // CB).astype(jnp.int32)
    col_index = (live_ids % CB).astype(jnp.int32)
    chosen = blocks[live_order].astype(jnp.float32)
    grouped = (chosen.reshape(NNZ // 16, 16, BLK, BLK), row_index.reshape(NNZ // 16, 16), col_index.reshape(NNZ // 16, 16))

    def forward_group(running, group_data):
        block_piece, rows_here, cols_here = group_data
        x_rows = x_blocks[:, rows_here, :].astype(jnp.float32)
        product = jnp.einsum('tgb,gbc->tgc', x_rows, block_piece, precision=lax.Precision.HIGHEST)
        return (running.at[:, cols_here, :].add(product), None)
    pre_three, unused = lax.scan(forward_group, jnp.zeros((TOKENS, CB, BLK), jnp.float32), grouped)
    pre_act = pre_three.reshape(TOKENS, FF_DEV)
    hidden = gelu_value(pre_act).astype(jnp.bfloat16)
    grad_pre = (grad_cols.astype(jnp.float32) * gelu_slope(pre_act)).astype(jnp.bfloat16)
    grad_three = grad_pre.reshape(TOKENS, CB, BLK)

    def backward_group(running, group_data):
        block_piece, rows_here, cols_here = group_data
        grad_piece = grad_three[:, cols_here, :].astype(jnp.float32)
        contrib = jnp.einsum('tgc,gbc->tgb', grad_piece, block_piece, precision=lax.Precision.HIGHEST)
        x_rows = x_groups[:, :, rows_here, :].astype(jnp.float32)
        group_grad = jnp.einsum('ntgb,ntgc->ngbc', x_rows, grad_piece.reshape(N_DP, TOK_DEV, 16, BLK), precision=lax.Precision.HIGHEST)
        group_grad = lax.optimization_barrier(group_grad.astype(jnp.bfloat16)).astype(jnp.float32)
        return (running.at[:, rows_here, :].add(contrib), lax.optimization_barrier(jnp.sum(group_grad, axis=0)))
    input_three, weight_parts = lax.scan(backward_group, jnp.zeros((TOKENS, RB, BLK), jnp.float32), grouped)
    partial_t = input_three.reshape(TOKENS, D).astype(jnp.bfloat16)
    summed = jnp.zeros((SLOTS, BLK, BLK), jnp.float32).at[live_order].set(weight_parts.reshape(NNZ, BLK, BLK))
    grad_blocks = (summed * (1.0 / math.sqrt(TOKENS))).astype(jnp.bfloat16)
    return (hidden, partial_t, grad_blocks)

def reference(inputs, grad_hidden, w_blocks, block_ids, counts):
    x_blocks = inputs.reshape(TOKENS, RB, BLK)
    x_groups = inputs.reshape(N_DP, TOK_DEV, RB, BLK)
    grad_shards = grad_hidden.reshape(TOKENS, N_TENSOR, FF_DEV).transpose(1, 0, 2)

    def one_shard(running, shard_data):
        blocks, ids_row, owner_counts, grad_cols = shard_data
        hidden, partial_t, grad_blocks = shard_pass(x_blocks, x_groups, blocks, ids_row, owner_counts, grad_cols)
        rounded = lax.optimization_barrier(partial_t).astype(jnp.float32)
        return (running + rounded, (hidden, grad_blocks))
    total, outputs = lax.scan(one_shard, jnp.zeros((TOKENS, D), jnp.float32), (w_blocks, block_ids, counts, grad_shards))
    hiddens, grad_blocks = outputs
    hidden = hiddens.transpose(1, 0, 2).reshape(TOKENS, FF)
    return (hidden, total.astype(jnp.bfloat16), grad_blocks)
```

```python
import functools
import math

import jax
import jax.numpy as jnp
from jax import lax
from jax.experimental import pallas as pl
from jax.experimental.pallas import tpu as pltpu
from jax.sharding import PartitionSpec as P

GELU_C = 0.7978845608028654
GELU_A = 0.044715
BLK = 128
CHUNK = 36
LAG = 2
UNROLL = 4
VMEM_BYTES = 56 * 1024 * 1024
F32 = jnp.float32
BF16 = jnp.bfloat16


def lane(index):
    return pl.ds(pl.multiple_of(index * BLK, BLK), BLK)


def resident(array):
    zeros = (0,) * len(array.shape)
    return pl.BlockSpec(array.shape, lambda *_: zeros, pipeline_mode=pl.Buffered(1))


def params():
    return pltpu.CompilerParams(vmem_limit_bytes=VMEM_BYTES)


def cost(microseconds):
    return pl.CostEstimate(flops=int(microseconds * 1e9), bytes_accessed=0, transcendentals=0)


def pack_kernel(source, span, own, sib, out):
    step = pl.program_id(0)
    chunk = out.shape[0]
    cap = own.shape[0]
    out[...] = jnp.zeros_like(out)

    def body(j, _):
        index = source[step * chunk + j]

        @pl.when(index < cap)
        def _():
            out[j] = own[index]

        @pl.when(index >= cap)
        def _():
            out[j] = sib[index - cap]

        return 0

    first = jnp.clip(span[0] - step * chunk, 0, chunk)
    lax.fori_loop(first, jnp.clip(span[1] - step * chunk, 0, chunk), body, 0)


def pack(source, span, own, sib):
    return pl.pallas_call(
        pack_kernel,
        grid_spec=pltpu.PrefetchScalarGridSpec(
            num_scalar_prefetch=2,
            grid=(source.shape[0] // CHUNK,),
            in_specs=[resident(own), resident(sib)],
            out_specs=pl.BlockSpec((CHUNK, BLK, BLK), lambda step, *_: (step, 0, 0)),
        ),
        out_shape=jax.ShapeDtypeStruct((source.shape[0], BLK, BLK), BF16),
        compiler_params=params(),
        name="pack",
    )(source, span, own, sib)


def accumulate(meta, arrays, one):
    for a, array in enumerate(arrays):

        def body(group, _, a=a, array=array):
            for u in range(UNROLL):
                j = group * UNROLL + u
                one(array[j], meta[a, 0] + j)
            return 0

        first = meta[a, 1] // UNROLL
        last = (meta[a, 2] + UNROLL - 1) // UNROLL
        lax.fori_loop(first, jnp.where(meta[a, 2] > meta[a, 1], last, first), body, 0)


def forward_kernel(count, first, last, rows, cols, meta, core, *refs):
    arrays, (x_own, x_sib, *refs) = refs[:count], refs[count:]
    if not first:
        pre_in, *refs = refs
    if last:
        gh_own, gh_sib, hidden_own, hidden_sib, grad_pre, pre = refs
    else:
        (pre,) = refs
    pre[...] = jnp.zeros_like(pre) if first else pre_in[...]
    tokens = x_own.shape[0]

    def one(block, position):
        r = lane(rows[position])
        left = jnp.concatenate([x_own[:, r], x_sib[:, r]], axis=0)
        pre[:, lane(cols[position])] += jnp.dot(left, block, preferred_element_type=F32)

    accumulate(meta, arrays, one)
    if last:

        def activate(c, _):
            s = lane(c)
            for t, gh, hidden in ((0, gh_own, hidden_own), (tokens, gh_sib, hidden_sib)):
                v = pre[t : t + tokens, s]
                sq = v * v
                th = jnp.tanh(GELU_C * (v + GELU_A * v * sq))
                hidden[:, s] = (0.5 * v * (1.0 + th)).astype(BF16)
                slope = 0.5 * (1.0 + th) + 0.5 * v * (1.0 - th * th) * GELU_C * (1.0 + 3.0 * GELU_A * sq)
                grad_pre[t : t + tokens, s] = (gh[:, s].astype(F32) * slope).astype(BF16)
            return 0

        lax.fori_loop(0, pre.shape[1] // BLK, activate, 0)


def forward(tables, meta, arrays, x, pre=None, gh=None):
    first, last = pre is None, gh is not None
    tokens, half_width = x[0].shape[0], gh[1].shape[1] if last else pre.shape[1] if pre is not None else tables[4]
    pre_shape = jax.ShapeDtypeStruct((2 * tokens, half_width), F32)
    inputs = [*arrays, *x] + ([] if first else [pre]) + (list(gh) if last else [])
    specs = [resident(a) for a in inputs]
    if last:
        specs[-2] = pl.BlockSpec((tokens, half_width), lambda i, rows, cols, meta, core: (0, core[0]), pipeline_mode=pl.Buffered(1))
        outs = [jax.ShapeDtypeStruct((n * tokens, half_width), BF16) for n in (1, 1, 2)]
    else:
        outs = [pre_shape]
    out = pl.pallas_call(
        functools.partial(forward_kernel, len(arrays), first, last),
        grid_spec=pltpu.PrefetchScalarGridSpec(
            num_scalar_prefetch=4,
            grid=(1,),
            in_specs=specs,
            out_specs=[resident(a) for a in outs],
            scratch_shapes=[pltpu.VMEM(pre_shape.shape, F32)] if last else [],
        ),
        out_shape=outs,
        input_output_aliases={} if first or last else {4 + len(arrays) + 2: 0},
        compiler_params=params(),
        cost_estimate=cost(20),
        name="forward_last" if last else "forward",
    )(tables[0], tables[1], meta, tables[2], *inputs)
    return out if last else out[0]


def input_grad_kernel(count, first, last, rows, cols, meta, *refs):
    arrays, (g, *refs) = refs[:count], refs[count:]
    if not first:
        total_in, *refs = refs
    if last:
        own, sib, total = refs
    else:
        (total,) = refs
    total[...] = jnp.zeros_like(total) if first else total_in[...]

    def one(block, position):
        product = lax.dot_general(
            g[:, lane(cols[position])], block, (((1,), (1,)), ((), ())), preferred_element_type=F32
        )
        total[:, lane(rows[position])] += product

    accumulate(meta, arrays, one)
    if last:
        tokens = own.shape[0]
        own[...] = total[:tokens, :].astype(BF16)
        sib[...] = total[tokens:, :].astype(BF16)


def input_grad(tables, meta, arrays, g, total=None, last=False):
    first = total is None
    inputs = [*arrays, g] + ([] if first else [total])
    total_shape = jax.ShapeDtypeStruct((g.shape[0], tables[3]), F32)
    outs = [jax.ShapeDtypeStruct((g.shape[0] // 2, tables[3]), BF16)] * 2 if last else [total_shape]
    out = pl.pallas_call(
        functools.partial(input_grad_kernel, len(arrays), first, last),
        grid_spec=pltpu.PrefetchScalarGridSpec(
            num_scalar_prefetch=3,
            grid=(1,),
            in_specs=[resident(a) for a in inputs],
            out_specs=[resident(a) for a in outs],
            scratch_shapes=[pltpu.VMEM(total_shape.shape, F32)] if last else [],
        ),
        out_shape=outs,
        input_output_aliases={} if first or last else {3 + len(arrays) + 1: 0},
        compiler_params=params(),
        cost_estimate=cost(25),
        name="input_grad_last" if last else "input_grad",
    )(tables[0], tables[1], meta, *inputs)
    return out if last else out[0]


def block_grad_kernel(rows, cols, which, xt, g, *refs):
    out = refs[-1]
    chunk = out.shape[0]
    step = pl.program_id(0)
    index = which[step]

    @pl.when((step == 0) | (index != which[jnp.maximum(step - 1, 0)]))
    def _():
        def body(group, _):
            for u in range(UNROLL):
                j = group * UNROLL + u
                position = index * chunk + j
                out[j] = jnp.dot(
                    xt[lane(rows[position]), :], g[:, lane(cols[position])], preferred_element_type=F32
                ).astype(BF16)
            return 0

        lax.fori_loop(0, chunk // UNROLL, body, 0)


def block_grad(rows, cols, which, xt, g, total, earlier=None):
    extra = [] if earlier is None else [earlier]
    return pl.pallas_call(
        block_grad_kernel,
        grid_spec=pltpu.PrefetchScalarGridSpec(
            num_scalar_prefetch=3,
            grid=(which.shape[0],),
            in_specs=[resident(xt), resident(g)] + [pl.BlockSpec(memory_space=pl.ANY)] * len(extra),
            out_specs=pl.BlockSpec((CHUNK, BLK, BLK), lambda step, rows, cols, which: (which[step], 0, 0)),
        ),
        out_shape=jax.ShapeDtypeStruct((total, BLK, BLK), BF16),
        input_output_aliases={5: 0} if extra else {},
        compiler_params=params(),
        cost_estimate=cost(12),
        name="block_grad",
    )(rows, cols, which, xt, g, *extra)


def collect_kernel(steps, scalars, meta, grads, *refs):
    arrays = refs[: 2 * steps]
    extra = refs[2 * steps : 2 * steps + 2]
    out, own, sums, sem = refs[2 * steps + 2 :]
    low, count, extras = scalars[0], scalars[1], scalars[2]

    def copy_own(i, _):
        pltpu.make_async_copy(grads.at[low + i], own.at[i], sem).start()
        return 0

    lax.fori_loop(0, count, copy_own, 0)

    def copy_range(source, side, a):
        def body(j, _):
            pltpu.make_async_copy(source(j), sums.at[side, meta[a, 0] + j - low], sem).start()
            return 0

        lax.fori_loop(meta[a, 1], meta[a, 2], body, 0)

    for a, array in enumerate(arrays):
        copy_range(lambda j, array=array: array.at[j], a % 2, a)

    def copy_extra(e, _):
        for side in range(2):
            copy_range(lambda j, side=side: extra[side].at[e, j], side, 2 * (steps + e) + side)
        return 0

    lax.fori_loop(0, extras, copy_extra, 0)

    def wait(i, _):
        pltpu.make_async_copy(grads.at[0], own.at[0], sem).wait()
        return 0

    lax.fori_loop(0, count * (1 + scalars[3] + scalars[4]), wait, 0)

    def add(i, _):
        total = own[i].astype(F32)
        left = jnp.where(scalars[3] > 0, sums[0, i].astype(F32), 0.0)
        right = jnp.where(scalars[4] > 0, sums[1, i].astype(F32), 0.0)
        out[i] = (total + left + right).astype(BF16)
        return 0

    lax.fori_loop(0, count, add, 0)


def collect(scalars, meta, grads, arrays, extra, size):
    anywhere = pl.BlockSpec(memory_space=pl.ANY)
    out = jax.ShapeDtypeStruct((size, BLK, BLK), BF16)
    return pl.pallas_call(
        functools.partial(collect_kernel, len(arrays) // 2),
        grid_spec=pltpu.PrefetchScalarGridSpec(
            num_scalar_prefetch=2,
            grid=(1,),
            in_specs=[anywhere] * (1 + len(arrays) + 2),
            out_specs=resident(out),
            scratch_shapes=[
                pltpu.VMEM((size, BLK, BLK), BF16),
                pltpu.VMEM((2, size, BLK, BLK), BF16),
                pltpu.SemaphoreType.DMA,
            ],
        ),
        out_shape=out,
        compiler_params=params(),
        cost_estimate=cost(6),
        name="collect",
    )(scalars, meta, grads, *arrays, *extra)


def finish_kernel(scale, where, mine, theirs, out):
    def body(s, _):
        index = where[1, s]
        block = jnp.where(where[0, s] > 0, mine[index], theirs[index]).astype(F32)
        out[s] = jnp.where(where[2, s] > 0, block * scale, 0.0).astype(BF16)
        return 0

    lax.fori_loop(0, out.shape[0], body, 0)


def finish(where, mine, theirs, scale):
    return pl.pallas_call(
        functools.partial(finish_kernel, scale),
        grid_spec=pltpu.PrefetchScalarGridSpec(
            num_scalar_prefetch=1,
            grid=(1,),
            in_specs=[resident(mine), resident(theirs)],
            out_specs=resident(mine),
        ),
        out_shape=jax.ShapeDtypeStruct(mine.shape, BF16),
        compiler_params=params(),
        name="finish",
    )(where, mine, theirs)


def unwritten(shape):
    return pl.pallas_call(
        lambda out: None,
        out_specs=pl.BlockSpec(memory_space=pl.ANY),
        out_shape=jax.ShapeDtypeStruct(shape, BF16),
        name="buffer",
    )()


def ceil_div(a, b):
    return (a + b - 1) // b


def per_device(inputs, grad_hidden, w_blocks, block_ids, counts):
    n_dp = lax.axis_size("dp")
    n_z = n_dp // 2
    me = lax.axis_index("dp")
    z, core = me // 2, me % 2
    tokens, width = inputs.shape
    hidden_width = grad_hidden.shape[1]
    half_width = hidden_width // 2
    col_blocks = hidden_width // BLK
    half_cols = col_blocks // 2
    cap = w_blocks.shape[1]
    live_total = cap * n_dp // 2
    total_chunks = -(-live_total // CHUNK)
    most_steps = max(-(-min((e + 1) * 2 * cap, live_total) // CHUNK) + LAG * (n_z - 2 - e) for e in range(n_z - 1))
    steps = max(3, min(most_steps - 1, -(-live_total // (2 * CHUNK)) + 1))
    spare = most_steps - steps
    to_right = [(d, d + 2) for d in range(n_dp - 2)]
    to_left = [(d + 2, d) for d in range(n_dp - 2)]
    swap = [(d, d ^ 1) for d in range(n_dp)]

    def exchange(value):
        return lax.ppermute(value, "dp", swap)

    def column_half(value, which):
        return lax.dynamic_slice_in_dim(value, which * half_width, half_width, 1)

    blocks = w_blocks[0]
    sib_blocks = exchange(blocks)
    small = lax.all_gather(jnp.concatenate([block_ids[0], counts[0]]), "dp", axis=0, tiled=False)
    slot = jnp.arange(cap, dtype=jnp.int32)
    ids = small[:, :cap]
    halves = jnp.where(slot < small[:, cap:], (ids % col_blocks) // half_cols, -1)
    per_chip = jnp.stack([jnp.sum(halves == h, axis=1).reshape(n_z, 2).sum(-1) for h in range(2)], axis=0)
    upto = jnp.arange(n_z)[:, None] <= jnp.arange(n_z)[None, :]
    ends = jnp.sum(jnp.where(upto, per_chip[..., None], 0), axis=1).astype(jnp.int32)
    edges = jnp.arange(n_z - 1, dtype=jnp.int32)
    cut = ends[..., :-1]
    right_steps = ceil_div(cut, CHUNK) + LAG * (n_z - 2 - edges)
    left_steps = ceil_div(ends[..., -1:], CHUNK) - cut // CHUNK + LAG * edges
    needed = jnp.max(jnp.maximum(right_steps, left_steps)).astype(jnp.int32)
    extras = jnp.maximum(needed - steps, 0)

    my_ends = ends[core]
    total = my_ends[-1]
    high = my_ends[z]
    low = jnp.where(z > 0, my_ends[jnp.maximum(z - 1, 0)], 0)
    used_chunks = ceil_div(total, CHUNK)

    member = halves == core
    owner_counts = jnp.sum(member, axis=1)
    owner_starts = jnp.sum(jnp.where(jnp.arange(n_dp)[:, None] < jnp.arange(n_dp)[None, :], owner_counts[:, None], 0), axis=0)
    earlier_slot = slot[:, None] < slot[None, :]
    rank = jnp.sum(member[:, :, None] & earlier_slot[None], axis=1)
    place = jnp.where(member, owner_starts[:, None] + rank, -1)
    tagged = (jnp.arange(n_dp * cap, dtype=jnp.int32).reshape(n_dp, cap) * 65536 + ids).reshape(1, -1)
    padded_total = total_chunks * CHUNK + CHUNK
    position = jnp.arange(padded_total, dtype=jnp.int32)
    table = jnp.sum(jnp.where(place.reshape(1, -1) == position[:, None], tagged, 0), axis=1)
    live_ids = table % 65536
    rows = live_ids // col_blocks
    cols = jnp.maximum(live_ids % col_blocks - core * half_cols, 0)

    local = jnp.arange(CHUNK + 2 * cap + CHUNK, dtype=jnp.int32) - CHUNK
    local = jnp.concatenate([local, jnp.full((-local.shape[0] % CHUNK,), -1, jnp.int32)])
    chip_place = lax.dynamic_slice_in_dim(place, 2 * z, 2, 0).reshape(1, -1)
    chip_slot = jnp.arange(2 * cap, dtype=jnp.int32)
    chip_slot = jnp.where(chip_slot // cap == core, 0, cap) + chip_slot % cap
    source = jnp.sum(jnp.where(chip_place == (low + local)[:, None], chip_slot[None, :] + 1, 0), axis=1) - 1
    source = jnp.where((local >= 0) & (local < high - low), source, -1).astype(jnp.int32)
    span = jnp.stack([jnp.full_like(low, CHUNK), high - low + CHUNK])
    packed = pack(source, span, blocks, sib_blocks)

    def own_chunk(q):
        start = jnp.clip(q * CHUNK - low + CHUNK, 0, 2 * cap + CHUNK)
        return lax.dynamic_slice(packed, (start, 0, 0), (CHUNK, BLK, BLK))

    def describe(q, first, last, valid):
        base = q * CHUNK
        valid = valid & (q >= 0) & (q < used_chunks)
        lo = jnp.where(valid, jnp.clip(first - base, 0, CHUNK), 0)
        hi = jnp.where(valid, jnp.clip(last - base, 0, CHUNK), 0)
        return jnp.stack([base, lo, jnp.maximum(lo, hi)], axis=-1)

    def gather_meta(v):
        right = describe(v - LAG * (n_z - 1 - z), 0, low, True)
        left = describe(used_chunks - 1 - (v - LAG * z), high, total, True)
        return jnp.stack([right, left], axis=-2).reshape(-1, 3).astype(jnp.int32)

    def scatter_meta(t, low, high):
        right = describe(used_chunks - 1 - (t - LAG * (z - 1)), low, high, z > 0)
        left = describe(t - LAG * (n_z - 2 - z), low, high, z < n_z - 1)
        return jnp.stack([right, left], axis=-2).reshape(-1, 3).astype(jnp.int32)

    def send(right, left):
        right, left = lax.optimization_barrier((right, left))
        got = lax.ppermute(right, "dp", to_right), lax.ppermute(left, "dp", to_left)
        return got, (right, left)

    def after(values, sent):
        return lax.optimization_barrier((values, sent))[0]

    def gather_step(v, old):
        right = own_chunk(v - LAG * (n_z - 2 - z))
        left = own_chunk(used_chunks - 1 - (v - LAG * (z - 1)))
        if old is not None:
            right, left = right + old[0], left + old[1]
        return send(right, left)

    empty = jnp.zeros((CHUNK, BLK, BLK), BF16)
    spare_shape = (spare, CHUNK, BLK, BLK)

    def gather_extra(i, carry):
        history, kept = carry
        got, _ = gather_step(needed - 1 - i, history[0])
        kept = tuple(lax.dynamic_update_index_in_dim(k, g, i, 0) for k, g in zip(kept, got))
        return (*history[1:], got), kept

    history = ((empty, empty),) * LAG
    history, kept = lax.fori_loop(
        0, extras, gather_extra, (history, (unwritten(spare_shape), unwritten(spare_shape)))
    )
    history = list(history)
    arrived, sent = [], None
    own_meta = jnp.stack([low - CHUNK, jnp.full_like(low, CHUNK), high - low + CHUNK])[None].astype(jnp.int32)
    metas = gather_meta(steps - 1 - jnp.arange(steps, dtype=jnp.int32))
    tables = (rows, cols, core.reshape(1).astype(jnp.int32), width, half_width)
    bounds = sorted({0, steps * 4 // 9, steps * 7 // 9, steps})
    batches = []
    for lo, hi in zip(bounds[:-1], bounds[1:]):
        for v in range(steps - 1 - lo, steps - 1 - hi, -1):
            old = history[-LAG]
            if sent is not None:
                old = after(old, sent)
            got, sent = gather_step(v, old)
            history.append(got)
            arrived.extend(got)
            if len(arrived) == 2:
                inputs, grad_hidden = after((inputs, grad_hidden), sent)
                x = (inputs, exchange(inputs))
                xt = jnp.concatenate([x[0].T, x[1].T], axis=1)
                gh = (grad_hidden, exchange(column_half(grad_hidden, 1 - core)))
        arrays, meta = arrived[2 * lo : 2 * hi], metas[2 * lo : 2 * hi]
        if lo == 0:
            arrays, meta = [packed, *arrays], jnp.concatenate([own_meta, meta])
            batches.append((meta, arrays))
            pre = forward(tables, meta, arrays, x)

            def forward_extra(i, running):
                pair = [lax.dynamic_index_in_dim(k, i, 0, keepdims=False) for k in kept]
                return forward(tables, gather_meta((needed - 1 - i)[None]), pair, x, running)

            pre = lax.fori_loop(0, extras, forward_extra, pre)
            continue
        batches.append((meta, arrays))
        if hi < steps:
            pre = forward(tables, meta, arrays, x, pre)
    hidden_own, hidden_sib, grad_pre = forward(tables, *batches[-1], x, pre, gh)

    top = used_chunks - 1
    pairs = [jnp.clip(jnp.stack([jnp.full_like(top, k), top - k]), 0, top).astype(jnp.int32) for k in range(LAG)]
    inner = jnp.arange(LAG, total_chunks, dtype=jnp.int32)
    inner = jnp.clip(jnp.minimum(inner, top - LAG), 0, top).astype(jnp.int32)
    grads = None

    def add(a, b):
        return (a.astype(F32) + b.astype(F32)).astype(BF16)

    def grad_chunk(buffer, q):
        start = jnp.clip(q, 0, total_chunks - 1) * CHUNK
        return lax.dynamic_slice(buffer, (start, 0, 0), (CHUNK, BLK, BLK))

    def scatter_step(t, old, buffer):
        right = grad_chunk(buffer, used_chunks - 1 - (t - LAG * z))
        left = grad_chunk(buffer, t - LAG * (n_z - 1 - z))
        if old is not None:
            right, left = add(right, old[0]), add(left, old[1])
        return send(right, left)

    history, sent = [], None
    last_meta = jnp.concatenate([meta for meta, _ in batches[1:]])
    last_arrays = [array for _, arrays in batches[1:] for array in arrays]
    for t in range(steps):
        old = history[-LAG] if t >= LAG else None
        if old is not None:
            old = after(old, sent)
        if t <= LAG:
            which = pairs[t] if t < LAG else inner
            if grads is not None:
                grads = after(grads, sent)
            grads = block_grad(rows, cols, which, xt, grad_pre, total_chunks * CHUNK, grads)
        got, sent = scatter_step(t, old, grads)
        history.append(got)
        if t == min(LAG, steps - 1):
            total_input = input_grad(tables, *batches[0], after(grad_pre, sent))
        if t == min(LAG + 2, steps - 1):
            total_input = after(total_input, sent)

            def input_extra(i, running):
                pair = [lax.dynamic_index_in_dim(k, i, 0, keepdims=False) for k in kept]
                return input_grad(tables, gather_meta((needed - 1 - i)[None]), pair, grad_pre, running)

            total_input = lax.fori_loop(0, extras, input_extra, total_input)
            input_own, input_sib = input_grad(tables, last_meta, last_arrays, grad_pre, total_input, last=True)
    sums = [array for pair in history for array in pair]
    partial_inputs = add(input_own, exchange(input_sib))
    grad_inputs = lax.psum_scatter(partial_inputs, "tensor", scatter_dimension=1, tiled=True)

    sib_hidden = exchange(hidden_sib)
    halves_hidden = [jnp.where(core == 0, hidden_own, sib_hidden), jnp.where(core == 0, sib_hidden, hidden_own)]
    hidden = jnp.concatenate(halves_hidden, axis=1)

    def scatter_extra(i, carry):
        history, kept = carry
        got, _ = scatter_step(steps + i, history[0], grads)
        kept = tuple(lax.dynamic_update_index_in_dim(k, g, i, 0) for k, g in zip(kept, got))
        return (*history[1:], got), kept

    _, kept_sums = lax.fori_loop(
        0, extras, scatter_extra, (tuple(history[-LAG:]), after(kept, input_sib))
    )
    def collected(owner):
        low, count = owner_starts[owner], owner_counts[owner]
        scalars = jnp.stack([low, count, extras, z > 0, z < n_z - 1]).astype(jnp.int32)
        meta = scatter_meta(jnp.arange(most_steps, dtype=jnp.int32), low, low + count)
        return collect(scalars, meta, grads, sums, kept_sums, cap)

    theirs = collected(me ^ 1)
    mine = collected(me)
    theirs = exchange(theirs)
    my_half = halves[me]
    my_rank = jnp.sum((my_half[:, None] == my_half[None, :]) & earlier_slot, axis=0)
    where = jnp.stack([my_half == core, my_rank, my_half >= 0]).astype(jnp.int32)
    grad_blocks = finish(where, mine, theirs, 1.0 / math.sqrt(tokens * n_dp))
    return hidden, grad_inputs, grad_blocks[None]


def solution(mesh):
    in_specs = (
        P("dp", None),
        P("dp", "tensor"),
        P("tensor", "dp", None, None),
        P("tensor", "dp"),
        P("tensor", "dp"),
    )
    out_specs = (P("dp", "tensor"), P("dp", "tensor"), P("tensor", "dp", None, None))
    return jax.shard_map(per_device, mesh=mesh, in_specs=in_specs, out_specs=out_specs, check_vma=False)
```

```python
import functools
import math

import jax
import jax.numpy as jnp
from jax import lax
from jax.experimental import pallas as pl
from jax.experimental.pallas import tpu as pltpu
from jax.sharding import PartitionSpec as P

GELU_C = 0.7978845608028654
GELU_A = 0.044715
BLK = 128
CHUNK = 36
LAG = 2
UNROLL = 4
VMEM_BYTES = 56 * 1024 * 1024
F32 = jnp.float32
BF16 = jnp.bfloat16


def lane(index):
    return pl.ds(pl.multiple_of(index * BLK, BLK), BLK)


def resident(array):
    zeros = (0,) * len(array.shape)
    return pl.BlockSpec(array.shape, lambda *_: zeros, pipeline_mode=pl.Buffered(1))


def params():
    return pltpu.CompilerParams(vmem_limit_bytes=VMEM_BYTES)


def cost(microseconds):
    return pl.CostEstimate(flops=int(microseconds * 1e9), bytes_accessed=0, transcendentals=0)


SMALL = cost(20)
TINY = cost(0.001)


def pack_kernel(source, span, own, sib, out):
    step = pl.program_id(0)
    chunk = out.shape[0]
    cap = own.shape[0]
    out[...] = jnp.zeros_like(out)

    def body(j, _):
        index = source[step * chunk + j]

        @pl.when(index < cap)
        def _():
            out[j] = own[index]

        @pl.when(index >= cap)
        def _():
            out[j] = sib[index - cap]

        return 0

    first = jnp.clip(span[0] - step * chunk, 0, chunk)
    lax.fori_loop(first, jnp.clip(span[1] - step * chunk, 0, chunk), body, 0)


def pack(source, span, own, sib):
    return pl.pallas_call(
        pack_kernel,
        grid_spec=pltpu.PrefetchScalarGridSpec(
            num_scalar_prefetch=2,
            grid=(source.shape[0] // CHUNK,),
            in_specs=[resident(own), resident(sib)],
            out_specs=pl.BlockSpec((CHUNK, BLK, BLK), lambda step, *_: (step, 0, 0)),
        ),
        out_shape=jax.ShapeDtypeStruct((source.shape[0], BLK, BLK), BF16),
        compiler_params=params(),
        name="pack",
    )(source, span, own, sib)


def accumulate(meta, extras, sources, kept, buffer, sem, one):
    def copy(k):
        array, start = sources[k]
        return pltpu.make_async_copy(array.at[pl.ds(start, CHUNK)], buffer.at[k % 2], sem.at[k % 2])

    def products(row, slot):
        def body(group, _):
            for u in range(UNROLL):
                j = group * UNROLL + u
                one(buffer[slot, j], meta[row, 0] + j)
            return 0

        lax.fori_loop(meta[row, 1] // UNROLL, (meta[row, 2] + UNROLL - 1) // UNROLL, body, 0)

    def if_any(row, step):
        pl.when(meta[row, 2] > meta[row, 1])(step)

    def use(k):
        copy(k).wait()
        products(k, k % 2)

    if_any(0, lambda: copy(0).start())
    for k in range(len(sources)):
        if k + 1 < len(sources):
            if_any(k + 1, lambda k=k: copy(k + 1).start())
        if_any(k, lambda k=k: use(k))

    if kept:

        def use_kept(e, _):
            for side in range(2):
                row = len(sources) + 2 * e + side

                def step(side=side, row=row):
                    arriving = pltpu.make_async_copy(kept[side].at[e], buffer.at[0], sem.at[0])
                    arriving.start()
                    arriving.wait()
                    products(row, 0)

                if_any(row, step)
            return 0

        lax.fori_loop(0, extras, use_kept, 0)


ANYWHERE = pl.BlockSpec(memory_space=pl.ANY)
BUFFERS = [pltpu.VMEM((2, CHUNK, BLK, BLK), BF16), pltpu.SemaphoreType.DMA((2,))]


def sources_of(refs, starts):
    return [(ref, start) for ref, where in zip(refs, starts) for start in where]


def forward_kernel(starts, first, last, rows, cols, meta, scalars, *refs):
    count = len(starts)
    sources, refs = sources_of(refs[:count], starts), refs[count:]
    kept = ()
    if first:
        kept, refs = refs[:2], refs[2:]
    x_own, x_sib, *refs = refs
    if not first:
        pre_in, *refs = refs
    if last:
        gh_own, gh_sib, hidden_own, hidden_sib, grad_pre, buffer, sem, pre = refs
    else:
        pre, buffer, sem = refs
    pre[...] = jnp.zeros_like(pre) if first else pre_in[...]
    tokens = x_own.shape[0]

    def one(block, position):
        r = lane(rows[position])
        left = jnp.concatenate([x_own[:, r], x_sib[:, r]], axis=0)
        pre[:, lane(cols[position])] += jnp.dot(left, block, preferred_element_type=F32)

    accumulate(meta, scalars[1], sources, kept, buffer, sem, one)
    if last:

        def activate(c, _):
            s = lane(c)
            for t, gh, hidden in ((0, gh_own, hidden_own), (tokens, gh_sib, hidden_sib)):
                v = pre[t : t + tokens, s]
                sq = v * v
                u = 0.5 + 0.5 * jnp.tanh(v * (GELU_C + GELU_C * GELU_A * sq))
                hidden[:, s] = (v * u).astype(BF16)
                bend = (v * (1.0 - u)) * (2.0 * GELU_C + 6.0 * GELU_C * GELU_A * sq)
                slope = u + u * bend
                grad_pre[t : t + tokens, s] = (gh[:, s].astype(F32) * slope).astype(BF16)
            return 0

        lax.fori_loop(0, pre.shape[1] // BLK, activate, 0)


def forward(tables, meta, arrays, starts, x, kept=None, pre=None, gh=None):
    first, last = pre is None, gh is not None
    tokens, half_width = x[0].shape[0], tables[4]
    pre_shape = jax.ShapeDtypeStruct((2 * tokens, half_width), F32)
    far = [*arrays, *(kept if first else ())]
    near = [*x] + ([] if first else [pre]) + (list(gh) if last else [])
    specs = [ANYWHERE] * len(far) + [resident(a) for a in near]
    if last:
        specs[-2] = pl.BlockSpec(
            (tokens, half_width), lambda i, rows, cols, meta, scalars: (0, scalars[0]), pipeline_mode=pl.Buffered(1)
        )
        outs = [jax.ShapeDtypeStruct((n * tokens, half_width), BF16) for n in (1, 1, 2)]
    else:
        outs = [pre_shape]
    out = pl.pallas_call(
        functools.partial(forward_kernel, starts, first, last),
        grid_spec=pltpu.PrefetchScalarGridSpec(
            num_scalar_prefetch=4,
            grid=(1,),
            in_specs=specs,
            out_specs=[resident(a) for a in outs],
            scratch_shapes=BUFFERS + ([pltpu.VMEM(pre_shape.shape, F32)] if last else []),
        ),
        out_shape=outs,
        input_output_aliases={} if first or last else {4 + len(arrays) + 2: 0},
        compiler_params=params(),
        cost_estimate=SMALL,
        name="forward_last" if last else "forward",
    )(tables[0], tables[1], meta, tables[2], *far, *near)
    return out if last else out[0]


def input_grad_kernel(starts, rows, cols, meta, scalars, *refs):
    count = len(starts)
    sources, kept = sources_of(refs[:count], starts), refs[count : count + 2]
    g, own, sib, buffer, sem, total = refs[count + 2 :]
    total[...] = jnp.zeros_like(total)

    def one(block, position):
        product = lax.dot_general(
            g[:, lane(cols[position])], block, (((1,), (1,)), ((), ())), preferred_element_type=F32
        )
        total[:, lane(rows[position])] += product

    accumulate(meta, scalars[1], sources, kept, buffer, sem, one)
    tokens = own.shape[0]
    own[...] = total[:tokens, :].astype(BF16)
    sib[...] = total[tokens:, :].astype(BF16)


def input_grad(tables, meta, arrays, starts, kept, g):
    tokens = g.shape[0] // 2
    return pl.pallas_call(
        functools.partial(input_grad_kernel, starts),
        grid_spec=pltpu.PrefetchScalarGridSpec(
            num_scalar_prefetch=4,
            grid=(1,),
            in_specs=[ANYWHERE] * (len(arrays) + 2) + [resident(g)],
            out_specs=[pl.BlockSpec((tokens, tables[3]), lambda *_: (0, 0), pipeline_mode=pl.Buffered(1))] * 2,
            scratch_shapes=BUFFERS + [pltpu.VMEM((2 * tokens, tables[3]), F32)],
        ),
        out_shape=[jax.ShapeDtypeStruct((tokens, tables[3]), BF16)] * 2,
        compiler_params=params(),
        cost_estimate=cost(50),
        name="input_grad",
    )(tables[0], tables[1], meta, tables[2], *arrays, *kept, g)


def block_grad_kernel(rows, cols, which, xt, g, *refs):
    out = refs[-1]
    chunk = out.shape[0]
    step = pl.program_id(0)
    index = which[step]

    @pl.when((step == 0) | (index != which[jnp.maximum(step - 1, 0)]))
    def _():
        def body(group, _):
            for u in range(UNROLL):
                j = group * UNROLL + u
                position = index * chunk + j
                out[j] = jnp.dot(
                    xt[lane(rows[position]), :], g[:, lane(cols[position])], preferred_element_type=F32
                ).astype(BF16)
            return 0

        lax.fori_loop(0, chunk // UNROLL, body, 0)


def block_grad(rows, cols, which, xt, g, total, earlier=None):
    extra = [] if earlier is None else [earlier]
    return pl.pallas_call(
        block_grad_kernel,
        grid_spec=pltpu.PrefetchScalarGridSpec(
            num_scalar_prefetch=3,
            grid=(which.shape[0],),
            in_specs=[resident(xt), resident(g)] + [pl.BlockSpec(memory_space=pl.ANY)] * len(extra),
            out_specs=pl.BlockSpec((CHUNK, BLK, BLK), lambda step, rows, cols, which: (which[step], 0, 0)),
        ),
        out_shape=jax.ShapeDtypeStruct((total, BLK, BLK), BF16),
        input_output_aliases={5: 0} if extra else {},
        compiler_params=params(),
        cost_estimate=SMALL,
        name="block_grad",
    )(rows, cols, which, xt, g, *extra)


def collect_kernel(steps, scale, scalars, meta, *refs):
    if scale is not None:
        where, *refs = refs
    grads, *refs = refs
    arrays = refs[: 2 * steps]
    extra = refs[2 * steps : 2 * steps + 2]
    refs = refs[2 * steps + 2 :]
    if scale is not None:
        theirs, *refs = refs
    out, own, sums, sem = refs
    low, count, extras = scalars[0], scalars[1], scalars[2]

    def copy_own(i, _):
        pltpu.make_async_copy(grads.at[low + i], own.at[i], sem).start()
        return 0

    lax.fori_loop(0, count, copy_own, 0)

    def copy_range(source, side, a):
        def body(j, _):
            pltpu.make_async_copy(source(j), sums.at[side, meta[a, 0] + j - low], sem).start()
            return 0

        lax.fori_loop(meta[a, 1], meta[a, 2], body, 0)

    for a, array in enumerate(arrays):
        copy_range(lambda j, array=array: array.at[j], a % 2, a)

    def copy_extra(e, _):
        for side in range(2):
            copy_range(lambda j, side=side: extra[side].at[e, j], side, 2 * (steps + e) + side)
        return 0

    lax.fori_loop(0, extras, copy_extra, 0)

    def wait(i, _):
        pltpu.make_async_copy(grads.at[0], own.at[0], sem).wait()
        return 0

    lax.fori_loop(0, count * (1 + scalars[3] + scalars[4]), wait, 0)

    def summed(i):
        left = jnp.where(scalars[3] > 0, sums[0, i].astype(F32), 0.0)
        right = jnp.where(scalars[4] > 0, sums[1, i].astype(F32), 0.0)
        return own[i].astype(F32) + left + right

    if scale is None:

        def add(i, _):
            out[i] = summed(i).astype(BF16)
            return 0

        lax.fori_loop(0, count, add, 0)
        return

    def fill(s, _):
        index = where[1, s]

        @pl.when(where[2, s] == 0)
        def _():
            out[s] = jnp.zeros((BLK, BLK), BF16)

        @pl.when((where[2, s] > 0) & (where[0, s] > 0))
        def _():
            out[s] = (summed(index) * scale).astype(BF16)

        @pl.when((where[2, s] > 0) & (where[0, s] == 0))
        def _():
            out[s] = (theirs[index].astype(F32) * scale).astype(BF16)

        return 0

    lax.fori_loop(0, out.shape[0], fill, 0)


def collect(scalars, meta, grads, arrays, extra, size, finish=None):
    anywhere = pl.BlockSpec(memory_space=pl.ANY)
    out = jax.ShapeDtypeStruct((size, BLK, BLK), BF16)
    where, theirs, scale = ([finish[0]], [finish[1]], finish[2]) if finish else ([], [], None)
    return pl.pallas_call(
        functools.partial(collect_kernel, len(arrays) // 2, scale),
        grid_spec=pltpu.PrefetchScalarGridSpec(
            num_scalar_prefetch=2 + len(where),
            grid=(1,),
            in_specs=[anywhere] * (1 + len(arrays) + 2) + [resident(a) for a in theirs],
            out_specs=resident(out),
            scratch_shapes=[
                pltpu.VMEM((size, BLK, BLK), BF16),
                pltpu.VMEM((2, size, BLK, BLK), BF16),
                pltpu.SemaphoreType.DMA,
            ],
        ),
        out_shape=out,
        compiler_params=params(),
        cost_estimate=TINY,
        name="finish" if finish else "collect",
    )(scalars, meta, *where, grads, *arrays, *extra, *theirs)


def unwritten(shape):
    return pl.pallas_call(
        lambda out: None,
        out_specs=pl.BlockSpec(memory_space=pl.ANY),
        out_shape=jax.ShapeDtypeStruct(shape, BF16),
        name="buffer",
    )()


def ceil_div(a, b):
    return (a + b - 1) // b


def per_device(inputs, grad_hidden, w_blocks, block_ids, counts):
    n_dp = lax.axis_size("dp")
    n_z = n_dp // 2
    me = lax.axis_index("dp")
    z, core = me // 2, me % 2
    tokens, width = inputs.shape
    hidden_width = grad_hidden.shape[1]
    half_width = hidden_width // 2
    col_blocks = hidden_width // BLK
    half_cols = col_blocks // 2
    cap = w_blocks.shape[1]
    live_total = cap * n_dp // 2
    total_chunks = -(-live_total // CHUNK)
    most_steps = max(-(-min((e + 1) * 2 * cap, live_total) // CHUNK) + LAG * (n_z - 2 - e) for e in range(n_z - 1))
    steps = min(most_steps, max(9, -(-live_total // (2 * CHUNK)) + 1))
    spare = max(1, most_steps - steps)
    to_right = [(d, d + 2) for d in range(n_dp - 2)]
    to_left = [(d + 2, d) for d in range(n_dp - 2)]
    swap = [(d, d ^ 1) for d in range(n_dp)]

    def exchange(value):
        return lax.ppermute(value, "dp", swap)

    def column_half(value, which):
        return lax.dynamic_slice_in_dim(value, which * half_width, half_width, 1)

    blocks = w_blocks[0]
    sib_blocks = exchange(blocks)
    small = lax.all_gather(jnp.concatenate([block_ids[0], counts[0]]), "dp", axis=0, tiled=False)
    slot = jnp.arange(cap, dtype=jnp.int32)
    ids = small[:, :cap]
    halves = jnp.where(slot < small[:, cap:], (ids % col_blocks) // half_cols, -1)
    per_chip = jnp.stack([jnp.sum(halves == h, axis=1).reshape(n_z, 2).sum(-1) for h in range(2)], axis=0)
    upto = jnp.arange(n_z)[:, None] <= jnp.arange(n_z)[None, :]
    ends = jnp.sum(jnp.where(upto, per_chip[..., None], 0), axis=1).astype(jnp.int32)
    edges = jnp.arange(n_z - 1, dtype=jnp.int32)
    cut = ends[..., :-1]
    right_steps = ceil_div(cut, CHUNK) + LAG * (n_z - 2 - edges)
    left_steps = ceil_div(ends[..., -1:], CHUNK) - cut // CHUNK + LAG * edges
    needed = jnp.max(jnp.maximum(right_steps, left_steps)).astype(jnp.int32)
    extras = jnp.maximum(needed - steps, 0)

    my_ends = ends[core]
    total = my_ends[-1]
    high = my_ends[z]
    low = jnp.where(z > 0, my_ends[jnp.maximum(z - 1, 0)], 0)
    used_chunks = ceil_div(total, CHUNK)

    member = halves == core
    owner_counts = jnp.sum(member, axis=1)
    owner_starts = jnp.sum(jnp.where(jnp.arange(n_dp)[:, None] < jnp.arange(n_dp)[None, :], owner_counts[:, None], 0), axis=0)
    earlier_slot = slot[:, None] < slot[None, :]
    rank = jnp.sum(member[:, :, None] & earlier_slot[None], axis=1)
    place = jnp.where(member, owner_starts[:, None] + rank, -1)
    tagged = (jnp.arange(n_dp * cap, dtype=jnp.int32).reshape(n_dp, cap) * 65536 + ids).reshape(1, -1)
    padded_total = total_chunks * CHUNK + CHUNK
    position = jnp.arange(padded_total, dtype=jnp.int32)
    table = jnp.sum(jnp.where(place.reshape(1, -1) == position[:, None], tagged, 0), axis=1)
    live_ids = table % 65536
    rows = live_ids // col_blocks
    cols = jnp.maximum(live_ids % col_blocks - core * half_cols, 0)

    local = jnp.arange(CHUNK + 2 * cap + CHUNK, dtype=jnp.int32) - CHUNK
    local = jnp.concatenate([local, jnp.full((-local.shape[0] % CHUNK,), -1, jnp.int32)])
    chip_place = lax.dynamic_slice_in_dim(place, 2 * z, 2, 0).reshape(1, -1)
    chip_slot = jnp.arange(2 * cap, dtype=jnp.int32)
    chip_slot = jnp.where(chip_slot // cap == core, 0, cap) + chip_slot % cap
    source = jnp.sum(jnp.where(chip_place == (low + local)[:, None], chip_slot[None, :] + 1, 0), axis=1) - 1
    source = jnp.where((local >= 0) & (local < high - low), source, -1).astype(jnp.int32)
    span = jnp.stack([jnp.full_like(low, CHUNK), high - low + CHUNK])
    packed = pack(source, span, blocks, sib_blocks)

    def own_chunk(q):
        start = jnp.clip(q * CHUNK - low + CHUNK, 0, 2 * cap + CHUNK)
        return lax.dynamic_slice(packed, (start, 0, 0), (CHUNK, BLK, BLK))

    def describe(q, first, last, valid):
        base = q * CHUNK
        valid = valid & (q >= 0) & (q < used_chunks)
        lo = jnp.where(valid, jnp.clip(first - base, 0, CHUNK), 0)
        hi = jnp.where(valid, jnp.clip(last - base, 0, CHUNK), 0)
        return jnp.stack([base, lo, jnp.maximum(lo, hi)], axis=-1)

    def gather_meta(v):
        right = describe(v - LAG * (n_z - 1 - z), 0, low, True)
        left = describe(used_chunks - 1 - (v - LAG * z), high, total, True)
        return jnp.stack([right, left], axis=-2).reshape(-1, 3).astype(jnp.int32)

    def scatter_meta(t, low, high):
        right = describe(used_chunks - 1 - (t - LAG * (z - 1)), low, high, z > 0)
        left = describe(t - LAG * (n_z - 2 - z), low, high, z < n_z - 1)
        return jnp.stack([right, left], axis=-2).reshape(-1, 3).astype(jnp.int32)

    def send(right, left):
        right, left = lax.optimization_barrier((right, left))
        got = lax.ppermute(right, "dp", to_right), lax.ppermute(left, "dp", to_left)
        return got, (right, left)

    def after(values, sent):
        return lax.optimization_barrier((values, sent))[0]

    def gather_step(v, old):
        right = own_chunk(v - LAG * (n_z - 2 - z))
        left = own_chunk(used_chunks - 1 - (v - LAG * (z - 1)))
        if old is not None:
            right, left = right + old[0], left + old[1]
        return send(right, left)

    spare_shape = (spare, CHUNK, BLK, BLK)

    def extra_arrival(kept, i):
        return tuple(
            jnp.where(i >= 0, lax.dynamic_index_in_dim(k, jnp.clip(i, 0, spare - 1), 0, keepdims=False), 0) for k in kept
        )

    def gather_extra(i, kept):
        got, _ = gather_step(needed - 1 - i, extra_arrival(kept, i - LAG))
        return tuple(lax.dynamic_update_index_in_dim(k, g, i, 0) for k, g in zip(kept, got))

    kept = lax.fori_loop(0, extras, gather_extra, (unwritten(spare_shape), unwritten(spare_shape)))
    history = []
    own_parts = -(-2 * cap // CHUNK)
    own_at = CHUNK * jnp.arange(own_parts, dtype=jnp.int32)
    own_meta = jnp.stack(
        [low + own_at, jnp.zeros_like(own_at), jnp.clip(high - low - own_at, 0, CHUNK)], axis=-1
    ).astype(jnp.int32)
    own_starts = tuple(CHUNK * (1 + k) for k in range(own_parts))
    metas = gather_meta(steps - 1 - jnp.arange(steps, dtype=jnp.int32))
    kept_meta = gather_meta(needed - 1 - jnp.arange(spare, dtype=jnp.int32))
    scalars = jnp.stack([core, extras]).astype(jnp.int32)
    tables = (rows, cols, scalars, width, half_width)
    arrived, sent = [], None
    early, late = steps * 4 // 9, steps * 7 // 9
    at_zero = ((0,),)
    for i in range(steps):
        old = history[i - LAG] if i >= LAG else extra_arrival(kept, extras - LAG + i)
        if sent is not None:
            old = after(old, (sent, gh) if i == 4 else sent)
        got, sent = gather_step(steps - 1 - i, old)
        history.append(got)
        arrived.extend(got)
        if i == 0:
            inputs, grad_hidden = after((inputs, grad_hidden), sent)
            x = (inputs, exchange(inputs))
            xt = jnp.concatenate([x[0].T, x[1].T], axis=1)
            gh = (grad_hidden, exchange(column_half(grad_hidden, 1 - core)))
    meta = jnp.concatenate([own_meta, metas[: 2 * early], kept_meta])
    pre = forward(tables, meta, [packed, *arrived[: 2 * early]], (own_starts, *(at_zero * 2 * early)), x, kept)
    span = slice(2 * early, 2 * late)
    pre = forward(tables, metas[span], arrived[span], at_zero * (2 * (late - early)), x, pre=pre)
    span = slice(2 * late, 2 * steps)
    hidden_own, hidden_sib, grad_pre = forward(
        tables, metas[span], arrived[span], at_zero * (2 * (steps - late)), x, pre=pre, gh=gh
    )

    top = used_chunks - 1
    pairs = [jnp.clip(jnp.stack([jnp.full_like(top, k), top - k]), 0, top).astype(jnp.int32) for k in range(LAG)]
    inner = jnp.arange(LAG, total_chunks, dtype=jnp.int32)
    inner = jnp.clip(jnp.minimum(inner, top - LAG), 0, top).astype(jnp.int32)
    grads = None

    def add(a, b):
        return (a.astype(F32) + b.astype(F32)).astype(BF16)

    def grad_chunk(buffer, q):
        start = jnp.clip(q, 0, total_chunks - 1) * CHUNK
        return lax.dynamic_slice(buffer, (start, 0, 0), (CHUNK, BLK, BLK))

    def owner_scalars(owner):
        low, count = owner_starts[owner], owner_counts[owner]
        scalars = jnp.stack([low, count, extras, z > 0, z < n_z - 1]).astype(jnp.int32)
        return scalars, scatter_meta(jnp.arange(most_steps, dtype=jnp.int32), low, low + count)

    my_half = halves[me]
    my_rank = jnp.sum((my_half[:, None] == my_half[None, :]) & earlier_slot, axis=0)
    where = jnp.stack([my_half == core, my_rank, my_half >= 0]).astype(jnp.int32)

    def scatter_step(t, old, buffer):
        right = grad_chunk(buffer, used_chunks - 1 - (t - LAG * z))
        left = grad_chunk(buffer, t - LAG * (n_z - 1 - z))
        if old is not None:
            right, left = add(right, old[0]), add(left, old[1])
        return send(right, left)

    history, sent, made = [], None, ()
    settled = {side: owner_scalars(me ^ side) for side in (0, 1)}
    for t in range(steps):
        old = history[-LAG] if t >= LAG else None
        if old is not None:
            old = after(old, (sent, made))
        if t <= LAG:
            which = pairs[t] if t < LAG else inner
            if grads is not None:
                grads = after(grads, sent)
            grads = block_grad(rows, cols, which, xt, grad_pre, total_chunks * CHUNK, grads)
        got, sent = scatter_step(t, old, grads)
        history.append(got)
        made = ()
        if t == 0:
            settled, where = after((settled, where), sent)
            made = settled, where
        if t == LAG + 1:
            meta = jnp.concatenate([own_meta, metas, kept_meta])
            starts = (own_starts, *(at_zero * (2 * steps)))
            input_own, input_sib = input_grad(
                tables, meta, [packed, *arrived], starts, kept, after(grad_pre, sent)
            )
        if t == LAG + 3:
            partial_inputs = add(input_own, exchange(after(input_sib, sent)))
        if t == steps - 2:
            made = partial_inputs
    sums = [array for pair in history for array in pair]
    grad_inputs = lax.psum_scatter(partial_inputs, "tensor", scatter_dimension=1, tiled=True)

    sib_hidden = exchange(hidden_sib)
    halves_hidden = [jnp.where(core == 0, hidden_own, sib_hidden), jnp.where(core == 0, sib_hidden, hidden_own)]
    hidden = jnp.concatenate(halves_hidden, axis=1)

    def scatter_extra(i, carry):
        history, kept = carry
        got, _ = scatter_step(steps + i, history[0], grads)
        kept = tuple(lax.dynamic_update_index_in_dim(k, g, i, 0) for k, g in zip(kept, got))
        return (*history[1:], got), kept

    _, kept_sums = lax.fori_loop(
        0, extras, scatter_extra, (tuple(history[-LAG:]), after(kept, input_sib))
    )
    theirs = exchange(collect(*settled[1], grads, sums, kept_sums, cap))
    scale = 1.0 / math.sqrt(tokens * n_dp)
    grad_blocks = collect(*settled[0], grads, sums, kept_sums, cap, (where, theirs, scale))
    return hidden, grad_inputs, grad_blocks[None]


def solution(mesh):
    in_specs = (
        P("dp", None),
        P("dp", "tensor"),
        P("tensor", "dp", None, None),
        P("tensor", "dp"),
        P("tensor", "dp"),
    )
    out_specs = (P("dp", "tensor"), P("dp", "tensor"), P("tensor", "dp", None, None))
    return jax.shard_map(per_device, mesh=mesh, in_specs=in_specs, out_specs=out_specs, check_vma=False)
```

```python
import functools
import math

import jax
import jax.numpy as jnp
from jax import lax
from jax.experimental import pallas as pl
from jax.experimental.pallas import tpu as pltpu
from jax.sharding import PartitionSpec as P

GELU_C = 0.7978845608028654
GELU_A = 0.044715
BLK = 128
CHUNK = 36
LAG = 2
UNROLL = 4
VMEM_BYTES = 56 * 1024 * 1024
F32 = jnp.float32
BF16 = jnp.bfloat16


def lane(index):
    return pl.ds(pl.multiple_of(index * BLK, BLK), BLK)


def resident(array):
    zeros = (0,) * len(array.shape)
    return pl.BlockSpec(array.shape, lambda *_: zeros, pipeline_mode=pl.Buffered(1))


def params():
    return pltpu.CompilerParams(vmem_limit_bytes=VMEM_BYTES)


def cost(microseconds):
    return pl.CostEstimate(flops=int(microseconds * 1e9), bytes_accessed=0, transcendentals=0)


SMALL = cost(20)
TINY = cost(0.001)


def pack_kernel(source, span, own, sib, out):
    step = pl.program_id(0)
    chunk = out.shape[0]
    cap = own.shape[0]
    out[...] = jnp.zeros_like(out)

    def body(j, _):
        index = source[step * chunk + j]

        @pl.when(index < cap)
        def _():
            out[j] = own[index]

        @pl.when(index >= cap)
        def _():
            out[j] = sib[index - cap]

        return 0

    first = jnp.clip(span[0] - step * chunk, 0, chunk)
    lax.fori_loop(first, jnp.clip(span[1] - step * chunk, 0, chunk), body, 0)


def pack(source, span, own, sib):
    return pl.pallas_call(
        pack_kernel,
        grid_spec=pltpu.PrefetchScalarGridSpec(
            num_scalar_prefetch=2,
            grid=(source.shape[0] // CHUNK,),
            in_specs=[resident(own), resident(sib)],
            out_specs=pl.BlockSpec((CHUNK, BLK, BLK), lambda step, *_: (step, 0, 0)),
        ),
        out_shape=jax.ShapeDtypeStruct((source.shape[0], BLK, BLK), BF16),
        compiler_params=params(),
        name="pack",
    )(source, span, own, sib)


def accumulate(meta, extras, sources, kept, buffer, sem, one):
    def copy(k):
        array, start = sources[k]
        return pltpu.make_async_copy(array.at[pl.ds(start, CHUNK)], buffer.at[k % 2], sem.at[k % 2])

    def products(row, slot):
        def body(group, _):
            for u in range(UNROLL):
                j = group * UNROLL + u
                one(buffer[slot, j], meta[row, 0] + j)
            return 0

        lax.fori_loop(meta[row, 1] // UNROLL, (meta[row, 2] + UNROLL - 1) // UNROLL, body, 0)

    def if_any(row, step):
        pl.when(meta[row, 2] > meta[row, 1])(step)

    def use(k):
        copy(k).wait()
        products(k, k % 2)

    if_any(0, lambda: copy(0).start())
    for k in range(len(sources)):
        if k + 1 < len(sources):
            if_any(k + 1, lambda k=k: copy(k + 1).start())
        if_any(k, lambda k=k: use(k))

    if kept:

        def use_kept(e, _):
            for side in range(2):
                row = len(sources) + 2 * e + side

                def step(side=side, row=row):
                    arriving = pltpu.make_async_copy(kept[side].at[e], buffer.at[0], sem.at[0])
                    arriving.start()
                    arriving.wait()
                    products(row, 0)

                if_any(row, step)
            return 0

        lax.fori_loop(0, extras, use_kept, 0)


ANYWHERE = pl.BlockSpec(memory_space=pl.ANY)
BUFFERS = [pltpu.VMEM((2, CHUNK, BLK, BLK), BF16), pltpu.SemaphoreType.DMA((2,))]


def sources_of(refs, starts):
    return [(ref, start) for ref, where in zip(refs, starts) for start in where]


def forward_kernel(starts, first, last, rows, cols, meta, scalars, *refs):
    count = len(starts)
    sources, refs = sources_of(refs[:count], starts), refs[count:]
    kept = ()
    if first:
        kept, refs = refs[:2], refs[2:]
    x_own, x_sib, *refs = refs
    if not first:
        pre_in, *refs = refs
    if last:
        gh_own, gh_sib, hidden_own, hidden_sib, grad_pre, buffer, sem, pre = refs
    else:
        pre, buffer, sem = refs
    pre[...] = jnp.zeros_like(pre) if first else pre_in[...]
    tokens = x_own.shape[0]

    def one(block, position):
        r = lane(rows[position])
        left = jnp.concatenate([x_own[:, r], x_sib[:, r]], axis=0)
        pre[:, lane(cols[position])] += jnp.dot(left, block, preferred_element_type=F32)

    accumulate(meta, scalars[1], sources, kept, buffer, sem, one)
    if last:

        def activate(c, _):
            s = lane(c)
            for t, gh, hidden in ((0, gh_own, hidden_own), (tokens, gh_sib, hidden_sib)):
                v = pre[t : t + tokens, s]
                sq = v * v
                u = 0.5 + 0.5 * jnp.tanh(v * (GELU_C + GELU_C * GELU_A * sq))
                hidden[:, s] = (v * u).astype(BF16)
                bend = (v * (1.0 - u)) * (2.0 * GELU_C + 6.0 * GELU_C * GELU_A * sq)
                slope = u + u * bend
                grad_pre[t : t + tokens, s] = (gh[:, s].astype(F32) * slope).astype(BF16)
            return 0

        lax.fori_loop(0, pre.shape[1] // BLK, activate, 0)


def forward(tables, meta, arrays, starts, x, kept=None, pre=None, gh=None):
    first, last = pre is None, gh is not None
    tokens, half_width = x[0].shape[0], tables[4]
    pre_shape = jax.ShapeDtypeStruct((2 * tokens, half_width), F32)
    far = [*arrays, *(kept if first else ())]
    near = [*x] + ([] if first else [pre]) + (list(gh) if last else [])
    specs = [ANYWHERE] * len(far) + [resident(a) for a in near]
    if last:
        specs[-2] = pl.BlockSpec(
            (tokens, half_width), lambda i, rows, cols, meta, scalars: (0, scalars[0]), pipeline_mode=pl.Buffered(1)
        )
        outs = [jax.ShapeDtypeStruct((n * tokens, half_width), BF16) for n in (1, 1, 2)]
    else:
        outs = [pre_shape]
    out = pl.pallas_call(
        functools.partial(forward_kernel, starts, first, last),
        grid_spec=pltpu.PrefetchScalarGridSpec(
            num_scalar_prefetch=4,
            grid=(1,),
            in_specs=specs,
            out_specs=[resident(a) for a in outs],
            scratch_shapes=BUFFERS + ([pltpu.VMEM(pre_shape.shape, F32)] if last else []),
        ),
        out_shape=outs,
        input_output_aliases={} if first or last else {4 + len(arrays) + 2: 0},
        compiler_params=params(),
        cost_estimate=SMALL,
        name="forward_last" if last else "forward",
    )(tables[0], tables[1], meta, tables[2], *far, *near)
    return out if last else out[0]


def input_grad_kernel(starts, rows, cols, meta, scalars, *refs):
    count = len(starts)
    sources, kept = sources_of(refs[:count], starts), refs[count : count + 2]
    g, out, buffer, sem, total = refs[count + 2 :]
    total[...] = jnp.zeros_like(total)

    def one(block, position):
        product = lax.dot_general(
            g[:, lane(cols[position])], block, (((1,), (1,)), ((), ())), preferred_element_type=F32
        )
        total[:, lane(rows[position])] += product

    accumulate(meta, scalars[1], sources, kept, buffer, sem, one)
    out[...] = total[...].astype(BF16)


def input_grad(tables, meta, arrays, starts, kept, g, side):
    tokens = g.shape[0] // 2
    return pl.pallas_call(
        functools.partial(input_grad_kernel, starts),
        grid_spec=pltpu.PrefetchScalarGridSpec(
            num_scalar_prefetch=4,
            grid=(1,),
            in_specs=[ANYWHERE] * (len(arrays) + 2)
            + [pl.BlockSpec((tokens, g.shape[1]), lambda *_: (side, 0), pipeline_mode=pl.Buffered(1))],
            out_specs=pl.BlockSpec((tokens, tables[3]), lambda *_: (0, 0), pipeline_mode=pl.Buffered(1)),
            scratch_shapes=BUFFERS + [pltpu.VMEM((tokens, tables[3]), F32)],
        ),
        out_shape=jax.ShapeDtypeStruct((tokens, tables[3]), BF16),
        compiler_params=params(),
        cost_estimate=cost(30),
        name="input_grad",
    )(tables[0], tables[1], meta, tables[2], *arrays, *kept, g)


def block_grad_kernel(rows, cols, which, xt, g, *refs):
    out = refs[-1]
    chunk = out.shape[0]
    step = pl.program_id(0)
    index = which[step]

    @pl.when((step == 0) | (index != which[jnp.maximum(step - 1, 0)]))
    def _():
        def body(group, _):
            for u in range(UNROLL):
                j = group * UNROLL + u
                position = index * chunk + j
                out[j] = jnp.dot(
                    xt[lane(rows[position]), :], g[:, lane(cols[position])], preferred_element_type=F32
                ).astype(BF16)
            return 0

        lax.fori_loop(0, chunk // UNROLL, body, 0)


def block_grad(rows, cols, which, xt, g, total, earlier=None):
    extra = [] if earlier is None else [earlier]
    return pl.pallas_call(
        block_grad_kernel,
        grid_spec=pltpu.PrefetchScalarGridSpec(
            num_scalar_prefetch=3,
            grid=(which.shape[0],),
            in_specs=[resident(xt), resident(g)] + [pl.BlockSpec(memory_space=pl.ANY)] * len(extra),
            out_specs=pl.BlockSpec((CHUNK, BLK, BLK), lambda step, rows, cols, which: (which[step], 0, 0)),
        ),
        out_shape=jax.ShapeDtypeStruct((total, BLK, BLK), BF16),
        input_output_aliases={5: 0} if extra else {},
        compiler_params=params(),
        cost_estimate=SMALL,
        name="block_grad",
    )(rows, cols, which, xt, g, *extra)


def collect_kernel(steps, scale, scalars, meta, *refs):
    if scale is not None:
        where, *refs = refs
    grads, *refs = refs
    arrays = refs[: 2 * steps]
    extra = refs[2 * steps : 2 * steps + 2]
    refs = refs[2 * steps + 2 :]
    if scale is not None:
        theirs, *refs = refs
    out, own, sums, sem = refs
    low, count, extras = scalars[0], scalars[1], scalars[2]

    def copy_own(i, _):
        pltpu.make_async_copy(grads.at[low + i], own.at[i], sem).start()
        return 0

    lax.fori_loop(0, count, copy_own, 0)

    def copy_range(source, side, a):
        def body(j, _):
            pltpu.make_async_copy(source(j), sums.at[side, meta[a, 0] + j - low], sem).start()
            return 0

        lax.fori_loop(meta[a, 1], meta[a, 2], body, 0)

    for a, array in enumerate(arrays):
        copy_range(lambda j, array=array: array.at[j], a % 2, a)

    def copy_extra(e, _):
        for side in range(2):
            copy_range(lambda j, side=side: extra[side].at[e, j], side, 2 * (steps + e) + side)
        return 0

    lax.fori_loop(0, extras, copy_extra, 0)

    def wait(i, _):
        pltpu.make_async_copy(grads.at[0], own.at[0], sem).wait()
        return 0

    lax.fori_loop(0, count * (1 + scalars[3] + scalars[4]), wait, 0)

    def summed(i):
        left = jnp.where(scalars[3] > 0, sums[0, i].astype(F32), 0.0)
        right = jnp.where(scalars[4] > 0, sums[1, i].astype(F32), 0.0)
        return own[i].astype(F32) + left + right

    if scale is None:

        def add(i, _):
            out[i] = summed(i).astype(BF16)
            return 0

        lax.fori_loop(0, count, add, 0)
        return

    def fill(s, _):
        index = where[1, s]

        @pl.when(where[2, s] == 0)
        def _():
            out[s] = jnp.zeros((BLK, BLK), BF16)

        @pl.when((where[2, s] > 0) & (where[0, s] > 0))
        def _():
            out[s] = (summed(index) * scale).astype(BF16)

        @pl.when((where[2, s] > 0) & (where[0, s] == 0))
        def _():
            out[s] = (theirs[index].astype(F32) * scale).astype(BF16)

        return 0

    lax.fori_loop(0, out.shape[0], fill, 0)


def collect(scalars, meta, grads, arrays, extra, size, finish=None):
    anywhere = pl.BlockSpec(memory_space=pl.ANY)
    out = jax.ShapeDtypeStruct((size, BLK, BLK), BF16)
    where, theirs, scale = ([finish[0]], [finish[1]], finish[2]) if finish else ([], [], None)
    return pl.pallas_call(
        functools.partial(collect_kernel, len(arrays) // 2, scale),
        grid_spec=pltpu.PrefetchScalarGridSpec(
            num_scalar_prefetch=2 + len(where),
            grid=(1,),
            in_specs=[anywhere] * (1 + len(arrays) + 2) + [resident(a) for a in theirs],
            out_specs=resident(out),
            scratch_shapes=[
                pltpu.VMEM((size, BLK, BLK), BF16),
                pltpu.VMEM((2, size, BLK, BLK), BF16),
                pltpu.SemaphoreType.DMA,
            ],
        ),
        out_shape=out,
        compiler_params=params(),
        cost_estimate=TINY,
        name="finish" if finish else "collect",
    )(scalars, meta, *where, grads, *arrays, *extra, *theirs)


def unwritten(shape):
    return pl.pallas_call(
        lambda out: None,
        out_specs=pl.BlockSpec(memory_space=pl.ANY),
        out_shape=jax.ShapeDtypeStruct(shape, BF16),
        name="buffer",
    )()


def ceil_div(a, b):
    return (a + b - 1) // b


def per_device(inputs, grad_hidden, w_blocks, block_ids, counts):
    n_dp = lax.axis_size("dp")
    n_z = n_dp // 2
    me = lax.axis_index("dp")
    z, core = me // 2, me % 2
    tokens, width = inputs.shape
    hidden_width = grad_hidden.shape[1]
    half_width = hidden_width // 2
    col_blocks = hidden_width // BLK
    half_cols = col_blocks // 2
    cap = w_blocks.shape[1]
    live_total = cap * n_dp // 2
    total_chunks = -(-live_total // CHUNK)
    most_steps = max(-(-min((e + 1) * 2 * cap, live_total) // CHUNK) + LAG * (n_z - 2 - e) for e in range(n_z - 1))
    steps = min(most_steps, max(9, -(-live_total // (2 * CHUNK)) + 1))
    spare = max(1, most_steps - steps)
    to_right = [(d, d + 2) for d in range(n_dp - 2)]
    to_left = [(d + 2, d) for d in range(n_dp - 2)]
    swap = [(d, d ^ 1) for d in range(n_dp)]

    def exchange(value):
        return lax.ppermute(value, "dp", swap)

    def column_half(value, which):
        return lax.dynamic_slice_in_dim(value, which * half_width, half_width, 1)

    blocks = w_blocks[0]
    sib_blocks = exchange(blocks)
    small = lax.all_gather(jnp.concatenate([block_ids[0], counts[0]]), "dp", axis=0, tiled=False)
    slot = jnp.arange(cap, dtype=jnp.int32)
    ids = small[:, :cap]
    halves = jnp.where(slot < small[:, cap:], (ids % col_blocks) // half_cols, -1)
    per_chip = jnp.stack([jnp.sum(halves == h, axis=1).reshape(n_z, 2).sum(-1) for h in range(2)], axis=0)
    upto = jnp.arange(n_z)[:, None] <= jnp.arange(n_z)[None, :]
    ends = jnp.sum(jnp.where(upto, per_chip[..., None], 0), axis=1).astype(jnp.int32)
    edges = jnp.arange(n_z - 1, dtype=jnp.int32)
    cut = ends[..., :-1]
    right_steps = ceil_div(cut, CHUNK) + LAG * (n_z - 2 - edges)
    left_steps = ceil_div(ends[..., -1:], CHUNK) - cut // CHUNK + LAG * edges
    needed = jnp.max(jnp.maximum(right_steps, left_steps)).astype(jnp.int32)
    extras = jnp.maximum(needed - steps, 0)

    my_ends = ends[core]
    total = my_ends[-1]
    high = my_ends[z]
    low = jnp.where(z > 0, my_ends[jnp.maximum(z - 1, 0)], 0)
    used_chunks = ceil_div(total, CHUNK)

    member = halves == core
    owner_counts = jnp.sum(member, axis=1)
    owner_starts = jnp.sum(jnp.where(jnp.arange(n_dp)[:, None] < jnp.arange(n_dp)[None, :], owner_counts[:, None], 0), axis=0)
    earlier_slot = slot[:, None] < slot[None, :]
    rank = jnp.sum(member[:, :, None] & earlier_slot[None], axis=1)
    place = jnp.where(member, owner_starts[:, None] + rank, -1)
    tagged = (jnp.arange(n_dp * cap, dtype=jnp.int32).reshape(n_dp, cap) * 65536 + ids).reshape(1, -1)
    padded_total = total_chunks * CHUNK + CHUNK
    position = jnp.arange(padded_total, dtype=jnp.int32)
    table = jnp.sum(jnp.where(place.reshape(1, -1) == position[:, None], tagged, 0), axis=1)
    live_ids = table % 65536
    rows = live_ids // col_blocks
    cols = jnp.maximum(live_ids % col_blocks - core * half_cols, 0)

    local = jnp.arange(CHUNK + 2 * cap + CHUNK, dtype=jnp.int32) - CHUNK
    local = jnp.concatenate([local, jnp.full((-local.shape[0] % CHUNK,), -1, jnp.int32)])
    chip_place = lax.dynamic_slice_in_dim(place, 2 * z, 2, 0).reshape(1, -1)
    chip_slot = jnp.arange(2 * cap, dtype=jnp.int32)
    chip_slot = jnp.where(chip_slot // cap == core, 0, cap) + chip_slot % cap
    source = jnp.sum(jnp.where(chip_place == (low + local)[:, None], chip_slot[None, :] + 1, 0), axis=1) - 1
    source = jnp.where((local >= 0) & (local < high - low), source, -1).astype(jnp.int32)
    span = jnp.stack([jnp.full_like(low, CHUNK), high - low + CHUNK])
    packed = pack(source, span, blocks, sib_blocks)

    def own_chunk(q):
        start = jnp.clip(q * CHUNK - low + CHUNK, 0, 2 * cap + CHUNK)
        return lax.dynamic_slice(packed, (start, 0, 0), (CHUNK, BLK, BLK))

    def describe(q, first, last, valid):
        base = q * CHUNK
        valid = valid & (q >= 0) & (q < used_chunks)
        lo = jnp.where(valid, jnp.clip(first - base, 0, CHUNK), 0)
        hi = jnp.where(valid, jnp.clip(last - base, 0, CHUNK), 0)
        return jnp.stack([base, lo, jnp.maximum(lo, hi)], axis=-1)

    def gather_meta(v):
        right = describe(v - LAG * (n_z - 1 - z), 0, low, True)
        left = describe(used_chunks - 1 - (v - LAG * z), high, total, True)
        return jnp.stack([right, left], axis=-2).reshape(-1, 3).astype(jnp.int32)

    def scatter_meta(t, low, high):
        right = describe(used_chunks - 1 - (t - LAG * (z - 1)), low, high, z > 0)
        left = describe(t - LAG * (n_z - 2 - z), low, high, z < n_z - 1)
        return jnp.stack([right, left], axis=-2).reshape(-1, 3).astype(jnp.int32)

    def send(right, left):
        right, left = lax.optimization_barrier((right, left))
        got = lax.ppermute(right, "dp", to_right), lax.ppermute(left, "dp", to_left)
        return got, (right, left)

    def after(values, sent):
        return lax.optimization_barrier((values, sent))[0]

    def gather_step(v, old):
        right = own_chunk(v - LAG * (n_z - 2 - z))
        left = own_chunk(used_chunks - 1 - (v - LAG * (z - 1)))
        if old is not None:
            right, left = right + old[0], left + old[1]
        return send(right, left)

    spare_shape = (spare, CHUNK, BLK, BLK)

    def extra_arrival(kept, i):
        return tuple(
            jnp.where(i >= 0, lax.dynamic_index_in_dim(k, jnp.clip(i, 0, spare - 1), 0, keepdims=False), 0) for k in kept
        )

    def gather_extra(i, kept):
        got, _ = gather_step(needed - 1 - i, extra_arrival(kept, i - LAG))
        return tuple(lax.dynamic_update_index_in_dim(k, g, i, 0) for k, g in zip(kept, got))

    kept = lax.fori_loop(0, extras, gather_extra, (unwritten(spare_shape), unwritten(spare_shape)))
    history = []
    own_parts = -(-2 * cap // CHUNK)
    own_at = CHUNK * jnp.arange(own_parts, dtype=jnp.int32)
    own_meta = jnp.stack(
        [low + own_at, jnp.zeros_like(own_at), jnp.clip(high - low - own_at, 0, CHUNK)], axis=-1
    ).astype(jnp.int32)
    own_starts = tuple(CHUNK * (1 + k) for k in range(own_parts))
    metas = gather_meta(steps - 1 - jnp.arange(steps, dtype=jnp.int32))
    kept_meta = gather_meta(needed - 1 - jnp.arange(spare, dtype=jnp.int32))
    scalars = jnp.stack([core, extras]).astype(jnp.int32)
    tables = (rows, cols, scalars, width, half_width)
    arrived, sent = [], None
    early, late = steps * 4 // 9, steps * 7 // 9
    at_zero = ((0,),)
    for i in range(steps):
        old = history[i - LAG] if i >= LAG else extra_arrival(kept, extras - LAG + i)
        if sent is not None:
            old = after(old, (sent, gh) if i == 4 else sent)
        got, sent = gather_step(steps - 1 - i, old)
        history.append(got)
        arrived.extend(got)
        if i == 0:
            inputs, grad_hidden = after((inputs, grad_hidden), sent)
            x = (inputs, exchange(inputs))
            xt = jnp.concatenate([x[0].T, x[1].T], axis=1)
            gh = (grad_hidden, exchange(column_half(grad_hidden, 1 - core)))
    meta = jnp.concatenate([own_meta, metas[: 2 * early], kept_meta])
    pre = forward(tables, meta, [packed, *arrived[: 2 * early]], (own_starts, *(at_zero * 2 * early)), x, kept)
    span = slice(2 * early, 2 * late)
    pre = forward(tables, metas[span], arrived[span], at_zero * (2 * (late - early)), x, pre=pre)
    span = slice(2 * late, 2 * steps)
    hidden_own, hidden_sib, grad_pre = forward(
        tables, metas[span], arrived[span], at_zero * (2 * (steps - late)), x, pre=pre, gh=gh
    )

    top = used_chunks - 1
    pairs = [jnp.clip(jnp.stack([jnp.full_like(top, k), top - k]), 0, top).astype(jnp.int32) for k in range(LAG)]
    inner = jnp.arange(LAG, total_chunks, dtype=jnp.int32)
    inner = jnp.clip(jnp.minimum(inner, top - LAG), 0, top).astype(jnp.int32)
    grads = None

    def add(a, b):
        return (a.astype(F32) + b.astype(F32)).astype(BF16)

    def grad_chunk(buffer, q):
        start = jnp.clip(q, 0, total_chunks - 1) * CHUNK
        return lax.dynamic_slice(buffer, (start, 0, 0), (CHUNK, BLK, BLK))

    def owner_scalars(owner):
        low, count = owner_starts[owner], owner_counts[owner]
        scalars = jnp.stack([low, count, extras, z > 0, z < n_z - 1]).astype(jnp.int32)
        return scalars, scatter_meta(jnp.arange(most_steps, dtype=jnp.int32), low, low + count)

    my_half = halves[me]
    my_rank = jnp.sum((my_half[:, None] == my_half[None, :]) & earlier_slot, axis=0)
    where = jnp.stack([my_half == core, my_rank, my_half >= 0]).astype(jnp.int32)

    def scatter_step(t, old, buffer):
        right = grad_chunk(buffer, used_chunks - 1 - (t - LAG * z))
        left = grad_chunk(buffer, t - LAG * (n_z - 1 - z))
        if old is not None:
            right, left = add(right, old[0]), add(left, old[1])
        return send(right, left)

    history, sent, made = [], None, ()
    settled = {side: owner_scalars(me ^ side) for side in (0, 1)}
    for t in range(steps):
        old = history[-LAG] if t >= LAG else None
        if old is not None:
            old = after(old, (sent, made))
        if t <= LAG:
            which = pairs[t] if t < LAG else inner
            if grads is not None:
                grads = after(grads, sent)
            grads = block_grad(rows, cols, which, xt, grad_pre, total_chunks * CHUNK, grads)
        got, sent = scatter_step(t, old, grads)
        history.append(got)
        made = ()
        if t == 0:
            settled, where = after((settled, where), sent)
            made = settled, where
        if t == LAG + 1:
            meta = jnp.concatenate([own_meta, metas, kept_meta])
            starts = (own_starts, *(at_zero * (2 * steps)))
            input_sib = input_grad(tables, meta, [packed, *arrived], starts, kept, after(grad_pre, sent), 1)
        if t == LAG + 3:
            input_own = input_grad(tables, meta, [packed, *arrived], starts, kept, after(grad_pre, sent), 0)
            partial_inputs = add(input_own, exchange(after(input_sib, sent)))
        if t == steps - 2:
            made = partial_inputs
    sums = [array for pair in history for array in pair]
    grad_inputs = lax.psum_scatter(partial_inputs, "tensor", scatter_dimension=1, tiled=True)

    sib_hidden = exchange(hidden_sib)
    halves_hidden = [jnp.where(core == 0, hidden_own, sib_hidden), jnp.where(core == 0, sib_hidden, hidden_own)]
    hidden = jnp.concatenate(halves_hidden, axis=1)

    def scatter_extra(i, carry):
        history, kept = carry
        got, _ = scatter_step(steps + i, history[0], grads)
        kept = tuple(lax.dynamic_update_index_in_dim(k, g, i, 0) for k, g in zip(kept, got))
        return (*history[1:], got), kept

    _, kept_sums = lax.fori_loop(
        0, extras, scatter_extra, (tuple(history[-LAG:]), after(kept, input_sib))
    )
    theirs = exchange(collect(*settled[1], grads, sums, kept_sums, cap))
    scale = 1.0 / math.sqrt(tokens * n_dp)
    grad_blocks = collect(*settled[0], grads, sums, kept_sums, cap, (where, theirs, scale))
    return hidden, grad_inputs, grad_blocks[None]


def solution(mesh):
    in_specs = (
        P("dp", None),
        P("dp", "tensor"),
        P("tensor", "dp", None, None),
        P("tensor", "dp"),
        P("tensor", "dp"),
    )
    out_specs = (P("dp", "tensor"), P("dp", "tensor"), P("tensor", "dp", None, None))
    return jax.shard_map(per_device, mesh=mesh, in_specs=in_specs, out_specs=out_specs, check_vma=False)
```
